32 devices in a mesh: grp: 1, ev: 32 (over z, y, x, core).
Axes of the slice: x: 2, y: 2, z: 4, core: 2. Of those that a mesh axis runs over, the one named last changes fastest.
Arguments:
- windows: bfloat16 [256, 3, 64, 1024], P(('grp', 'ev')), may hold values from -400 to 400, as said below
- rotation: bfloat16 [256, 3, 64], P(('grp', 'ev')), may hold values from -3 to 3
- source_inverse: bfloat16 [256, 1024], P(('grp', 'ev')), may hold values from -3.4 to 3.4
- send_rows: int32 [1024, 64], P(('grp', 'ev')), may hold values from 0 to 511, as said below
- tile_station: int32 [2048], P(('grp', 'ev')), may hold values from 0 to 63, as said below
- tile_count: int32 [2048], P(('grp', 'ev')), may hold values from 16 to 128
- pair_rows: int32 [2, 262144], P(None, ('grp', 'ev')), may hold values from 0 to 2047, as said below
Outputs:
- correlation: float32 [262144, 255], P(('grp', 'ev'))
The draws below stay inside these ranges and needn't reach their ends.
Inputs may be any that keep to these rules, and one draw needn't show every extreme that they name: Each event's windows carry a scale of their own, and each station's another. `send_rows`: row j of the block of device o names the rows of device o sent to device j, each as local event times 64 plus station, with the station of the tile whose residue matches the receiving slot (o * 64 + k) mod 64. `tile_station`: tile t of a device is fed by received slots r with r mod 64 = t mod 64, all at the tile's station. `pair_rows`: entries count the rows a device receives by sending device then slot; both members of a slot lie at its tile's station.
All inputs are finite; a program needn't handle non-finite values.
Results may differ from the reference program's by a relative error of at most 0.007.
Values may be sent and summed in bfloat16 or wider, within the bound.
A program may use at most 64 MiB of HBM per device.

```python
import math
from functools import partial
import jax
import jax.numpy as jnp
from jax import lax

NS = 1024
LAGS = 255
STA = 64
TILE_PAIRS = 128
EV_DEV = 8
TILES_DEV = 64
SLOTS_DEV = 2048
PEERS = 32
EVENTS = 256
TILES = 2048
PAIRS_DEV = 8192
PAIRS = 262144
CAP = 64


def route_tables(key):
    base_key = jax.random.fold_in(key, 501)
    capacity = SLOTS_DEV // PEERS
    stations = jax.random.randint(jax.random.fold_in(base_key, 1), (PEERS, TILES_DEV), 0, STA)
    stations = stations.at[0, 0].set(STA - 1)
    stations = stations.at[1, 0].set(0)
    source = jnp.arange(PEERS, dtype=jnp.int32)[:, None, None]
    slot_index = jnp.arange(capacity, dtype=jnp.int32)[None, None, :]
    column = (source * capacity + slot_index) % TILES_DEV
    target = jnp.arange(PEERS, dtype=jnp.int32)[None, :, None]
    station_ids = stations[target, column]
    event_ids = jax.random.randint(jax.random.fold_in(base_key, 2), (PEERS, PEERS, capacity), 0, EV_DEV)
    event_ids = event_ids.at[0, 0, 0].set(EV_DEV - 1)
    event_ids = event_ids.at[0, 1, 0].set(0)
    send_table = (event_ids * STA + station_ids).reshape(PEERS * PEERS, capacity).astype(jnp.int32)
    picked = jax.random.randint(jax.random.fold_in(base_key, 3), (2, PEERS, TILES_DEV, TILE_PAIRS), 0, SLOTS_DEV // TILES_DEV)
    tile_ids = jnp.arange(TILES_DEV, dtype=jnp.int32)[None, None, :, None]
    pair_slots = tile_ids + TILES_DEV * picked
    pair_slots = pair_slots.at[0, :, 0, 0].set(0)
    pair_slots = pair_slots.at[1, :, TILES_DEV - 1, 0].set(SLOTS_DEV - 1)
    return (stations.reshape(TILES).astype(jnp.int32), send_table, pair_slots.reshape(2, PAIRS).astype(jnp.int32))


def draw_send_rows(key, part):
    return route_tables(key)[1]


def draw_tile_station(key, part):
    return route_tables(key)[0]


def draw_pair_rows(key, part):
    return route_tables(key)[2]


def draw_windows(key, part):
    base_key = jax.random.fold_in(key, 11)
    gauss_part = jnp.clip(jax.random.normal(jax.random.fold_in(base_key, 1), (EVENTS, 3, STA, NS), jnp.float32), -5.0, 5.0)
    position = jnp.arange(EVENTS, dtype=jnp.float32) / max(EVENTS - 1, 1)
    station_gain = jnp.exp(jax.random.uniform(jax.random.fold_in(base_key, 2), (STA,), jnp.float32, 0.0, 1.1))
    growth = jnp.sqrt(1.0 + 2.0 * position)
    spread = jnp.exp(jax.random.uniform(jax.random.fold_in(base_key, 3), (EVENTS,), jnp.float32, 0.0, 1.15))
    amplitude = (growth * spread)[:, None, None, None] * station_gain[None, None, :, None]
    return (gauss_part * amplitude).astype(jnp.bfloat16)


def draw_source_inverse(key, part):
    base_key = jax.random.fold_in(key, 23)
    magnitude = jnp.exp(jax.random.uniform(jax.random.fold_in(base_key, 1), (EVENTS, NS // 2), jnp.float32, -0.7, 0.7))
    angles = jax.random.uniform(jax.random.fold_in(base_key, 2), (EVENTS, NS // 2), jnp.float32, -math.pi, math.pi)
    return jnp.concatenate([magnitude * jnp.cos(angles), magnitude * jnp.sin(angles)], axis=1).astype(jnp.bfloat16)


def set_ends(values, stream_key, least, largest):
    longest = values.shape.index(max(values.shape))
    spots = []
    for shift in (0, 1):
        where = [jax.random.randint(jax.random.fold_in(stream_key, axis), (), 0, length) for axis, length in enumerate(values.shape)]
        where[longest] = (where[longest] + shift) % values.shape[longest]
        spots.append(tuple(where))
    return values.at[spots[0]].set(least).at[spots[1]].set(largest)


def levels(stream_key, shape, cuts, least, top_value):
    level = 1.0
    for dim, shards_of in cuts:
        steps = jax.random.uniform(jax.random.fold_in(jax.random.fold_in(stream_key, 6), dim), (shards_of,), jnp.float32, least / len(cuts), top_value / len(cuts))
        level = level * jnp.repeat(jnp.exp(steps), shape[dim] // shards_of).reshape((-1,) + (1,) * (len(shape) - 1 - dim))
    return level


def bell_draw(own_key, extent, deviation, bound, split=(), held_as=jnp.bfloat16):
    loudness = levels(own_key, extent, split, -0.22, 0.18) if split else 1.0
    drawn = jax.random.normal(own_key, extent, jnp.float32) * deviation * loudness
    return jnp.minimum(jnp.maximum(drawn, -bound), bound).astype(held_as)


def setup_inputs(seed: int = 0, part: int = 0) -> dict:
    arg_keys = jax.random.split(jax.random.key(seed), 8)
    part_keys = jax.random.split(jax.random.fold_in(arg_keys[7], part), 8)
    windows = draw_windows(jax.random.fold_in(jax.random.fold_in(arg_keys[7], part), 71), part)
    rotation = bell_draw(part_keys[1], (EVENTS, 3, STA), 0.6, 3.0, ((0, 32),))
    source_inverse = draw_source_inverse(jax.random.fold_in(jax.random.fold_in(arg_keys[7], part), 71), part)
    send_rows = draw_send_rows(jax.random.fold_in(jax.random.fold_in(arg_keys[7], part), 71), part)
    tile_station = draw_tile_station(jax.random.fold_in(jax.random.fold_in(arg_keys[7], part), 71), part)
    tile_count = set_ends(jax.random.randint(part_keys[5], (TILES,), TILE_PAIRS // 8, TILE_PAIRS + 1), jax.random.fold_in(part_keys[5], 1), TILE_PAIRS // 8, TILE_PAIRS).astype(jnp.int32)
    pair_rows = draw_pair_rows(jax.random.fold_in(jax.random.fold_in(arg_keys[7], part), 71), part)
    return {"windows": windows, "rotation": rotation, "source_inverse": source_inverse, "send_rows": send_rows, "tile_station": tile_station, "tile_count": tile_count, "pair_rows": pair_rows}


epsilon = 1e-06

def spectral_table(length):
    half_len = length // 2
    samples = jnp.arange(length, dtype=jnp.int32)[:, None]
    frequency = jnp.arange(half_len, dtype=jnp.int32)[None, :]
    angles = (samples * frequency % length).astype(jnp.float32) * (2.0 * math.pi / length)
    factor = 1.0 / math.sqrt(length)
    return jnp.concatenate([jnp.cos(angles) * factor, -jnp.sin(angles) * factor], axis=1).astype(jnp.bfloat16)

def lag_table(length, lag_count):
    half_len = length // 2
    frequency = jnp.arange(half_len, dtype=jnp.int32)[:, None]
    shifts = jnp.arange(lag_count, dtype=jnp.int32)[None, :] - lag_count // 2
    angles = (frequency * shifts % length).astype(jnp.float32) * (2.0 * math.pi / length)
    factor = 1.0 / math.sqrt(half_len)
    return jnp.concatenate([jnp.cos(angles) * factor, -jnp.sin(angles) * factor], axis=0).astype(jnp.bfloat16)

def event_spectra(windows, rotation, source_inverse, dft_table):
    half_len = dft_table.shape[1] // 2
    transverse = lax.optimization_barrier(jnp.sum(rotation.astype(jnp.float32)[..., None] * windows.astype(jnp.float32), axis=1)).astype(jnp.bfloat16)
    events, stations, length = transverse.shape
    spectrum = jnp.dot(transverse.reshape(events * stations, length), dft_table, preferred_element_type=jnp.float32)
    spectrum = spectrum.reshape(events, stations, length)
    filter_gain = source_inverse.astype(jnp.float32)[:, None, :]
    real_in, imag_in = (spectrum[..., :half_len], spectrum[..., half_len:])
    real_gain, imag_gain = (filter_gain[..., :half_len], filter_gain[..., half_len:])
    return jnp.concatenate([real_in * real_gain - imag_in * imag_gain, real_in * imag_gain + imag_in * real_gain], axis=-1)

def correlate_group(spectra, lag_tab, tile_pairs, pieces):
    first_rows, second_rows, weights, counts = pieces
    half_len = spectra.shape[1] // 2
    first_spec = spectra[first_rows].astype(jnp.float32)
    second_spec = spectra[second_rows].astype(jnp.float32)
    first_re, first_im = (first_spec[:, :half_len], first_spec[:, half_len:])
    second_re, second_im = (second_spec[:, :half_len], second_spec[:, half_len:])
    row_weight = jnp.repeat(weights, tile_pairs, axis=0)
    cross_spec = jnp.concatenate([(first_re * second_re + first_im * second_im) * row_weight, (first_im * second_re - first_re * second_im) * row_weight], axis=1).astype(jnp.bfloat16)
    lagged = jnp.dot(cross_spec, lag_tab, preferred_element_type=jnp.float32)
    live_rows = jnp.arange(lagged.shape[0], dtype=jnp.int32) % tile_pairs < jnp.repeat(counts, tile_pairs)
    return jnp.where(live_rows[:, None], lagged, jnp.zeros_like(lagged))

def reference(windows, rotation, source_inverse, send_rows, tile_station, tile_count, pair_rows):
    events, components, stations, length = windows.shape
    half_len = length // 2
    dft_table = spectral_table(length)

    def per_owner(pieces):
        deconvolved = event_spectra(pieces[0], pieces[1], pieces[2], dft_table)
        power_part = lax.optimization_barrier(jnp.sum(deconvolved[..., :half_len] ** 2 + deconvolved[..., half_len:] ** 2, axis=0))
        return (deconvolved.astype(jnp.bfloat16), power_part)
    shaped = (windows.reshape(PEERS, EV_DEV, components, stations, length), rotation.reshape(PEERS, EV_DEV, components, stations), source_inverse.reshape(PEERS, EV_DEV, length))
    spectra, powers = lax.map(per_owner, shaped)
    power_sum = lax.optimization_barrier(jnp.sum(powers, axis=0))
    weight = 1.0 / (power_sum / events + epsilon)
    spectra = spectra.reshape(events * stations, length)
    pair_total = pair_rows.shape[1]
    device = jnp.arange(pair_total, dtype=jnp.int32) // PAIRS_DEV
    source = pair_rows // CAP
    slot_index = pair_rows % CAP
    local_row = send_rows[source * PEERS + device[None, :], slot_index]
    row_ids = (source * (EV_DEV * stations) + local_row).astype(jnp.int32)
    onehot = (tile_station[:, None] == jnp.arange(stations, dtype=jnp.int32)[None, :]).astype(jnp.float32)
    tile_weight = jnp.dot(onehot, weight, precision=lax.Precision.HIGHEST)
    groups = tile_station.shape[0] // 4
    group_rows = 4 * TILE_PAIRS
    correlate = partial(correlate_group, spectra, lag_table(length, LAGS), TILE_PAIRS)
    result = lax.map(correlate, (row_ids[0].reshape(groups, group_rows), row_ids[1].reshape(groups, group_rows), tile_weight.reshape(groups, 4, half_len), tile_count.reshape(groups, 4)))
    return result.reshape(pair_total, LAGS)
```

```python
from functools import partial
import math

import jax
import jax.numpy as jnp
import numpy as np
from jax import lax
from jax.experimental import pallas as pl
from jax.experimental.pallas import tpu as pltpu
from jax.sharding import PartitionSpec as P

LAGS = 255
GROUP = 8
epsilon = 1e-06


def spectral_table(length):
    half_len = length // 2
    samples = np.arange(length, dtype=np.int32)[:, None]
    frequency = np.arange(half_len, dtype=np.int32)[None, :]
    angles = (samples * frequency % length).astype(np.float32) * np.float32(2.0 * math.pi / length)
    factor = np.float32(1.0 / math.sqrt(length))
    return jnp.asarray(
        np.concatenate([np.cos(angles) * factor, -np.sin(angles) * factor], axis=1), jnp.bfloat16
    )


def lag_table(length, lag_count):
    half_len = length // 2
    frequency = np.arange(half_len, dtype=np.int32)[:, None]
    shifts = np.arange(lag_count, dtype=np.int32)[None, :] - lag_count // 2
    angles = (frequency * shifts % length).astype(np.float32) * np.float32(2.0 * math.pi / length)
    factor = np.float32(1.0 / math.sqrt(half_len))
    return jnp.asarray(
        np.concatenate([np.cos(angles) * factor, -np.sin(angles) * factor], axis=0), jnp.bfloat16
    )


def exchange_kernel(
    n, events_total, win_ref, rot_ref, inv_ref, send_ref, table_ref,
    recv_ref, weight_ref,
    spectra, power, msg, part_out, part_in, w_in,
    send_sem, recv_sem, psend, precv, wsend, wrecv, local_sem,
):
    me = lax.axis_index("ev")
    grp = lax.axis_index("grp")
    mesh_id = pl.DeviceIdType.MESH
    ev_dev, comps, stations, length = win_ref.shape
    half = length // 2
    cap = recv_ref.shape[1]
    own = stations // n
    peers = range(1, n)

    barrier = pltpu.get_barrier_semaphore()

    @pl.loop(1, n)
    def _(s):
        pl.semaphore_signal(
            barrier, inc=1, device_id=(grp, lax.rem(me + s, n)), device_id_type=mesh_id
        )

    power[...] = jnp.zeros_like(power)
    diag = lax.broadcasted_iota(jnp.int32, (stations, stations), 0) == lax.broadcasted_iota(
        jnp.int32, (stations, stations), 1
    )
    inv_all = inv_ref[...].astype(jnp.float32)
    event_id = lax.broadcasted_iota(jnp.int32, (ev_dev, length), 0)

    @pl.loop(0, ev_dev)
    def _(e):
        rot = rot_ref[e].astype(jnp.float32)
        acc = None
        for c in range(comps):
            col = jnp.sum(
                jnp.where(diag, jnp.broadcast_to(rot[c : c + 1, :], diag.shape), 0.0),
                axis=1, keepdims=True,
            )
            term = col * win_ref[e, c].astype(jnp.float32)
            acc = term if acc is None else acc + term
        spec = jnp.dot(
            acc.astype(jnp.bfloat16), table_ref[...], preferred_element_type=jnp.float32
        )
        gain = jnp.sum(jnp.where(event_id == e, inv_all, 0.0), axis=0, keepdims=True)
        re, im = spec[:, :half], spec[:, half:]
        g_re, g_im = gain[:, :half], gain[:, half:]
        d_re = re * g_re - im * g_im
        d_im = re * g_im + im * g_re
        power[...] += d_re * d_re + d_im * d_im
        row = pl.multiple_of(e * stations, stations)
        spectra[pl.ds(row, stations), :half] = d_re.astype(jnp.bfloat16)
        spectra[pl.ds(row, stations), half:] = d_im.astype(jnp.bfloat16)

    pl.semaphore_wait(barrier, n - 1)

    for j in range(n):
        part_out[j] = power[j * own : (j + 1) * own, :]

    def part_copy(s):
        return pltpu.make_async_remote_copy(
            src_ref=part_out.at[lax.rem(me + s, n)], dst_ref=part_in.at[s],
            send_sem=psend.at[s], recv_sem=precv.at[s],
            device_id=(grp, lax.rem(me + s, n)), device_id_type=mesh_id,
        )

    @pl.loop(1, n)
    def _(s):
        part_copy(s).start()

    def msg_copy(s):
        target = lax.rem(me + s, n)
        return pltpu.make_async_remote_copy(
            src_ref=msg.at[target], dst_ref=recv_ref.at[me],
            send_sem=send_sem.at[s], recv_sem=recv_sem.at[s],
            device_id=(grp, target), device_id_type=mesh_id,
        )

    rows = ev_dev * stations
    row_id = lax.broadcasted_iota(jnp.int32, (rows, GROUP * cap), 0)

    @pl.loop(0, n // GROUP)
    def _(g):
        pick = (row_id == send_ref[pl.ds(g, 1), :]).astype(jnp.float32).astype(jnp.bfloat16)
        got = lax.dot_general(
            pick, spectra[...], (((0,), (0,)), ((), ())), preferred_element_type=jnp.float32
        )
        msg[pl.ds(pl.multiple_of(g * GROUP, GROUP), GROUP)] = got.astype(jnp.bfloat16).reshape(
            GROUP, cap, length
        )

    own_copy = pltpu.make_async_copy(msg.at[me], recv_ref.at[me], local_sem)
    own_copy.start()

    @pl.loop(1, n)
    def _(s):
        part_copy(s).wait_recv()

    total = part_out[me]
    for s in peers:
        total = total + part_in[s]
    w_own = 1.0 / (total / events_total + epsilon)
    w_in[0] = w_own

    def w_copy(s):
        return pltpu.make_async_remote_copy(
            src_ref=w_in.at[0], dst_ref=w_in.at[s],
            send_sem=wsend.at[s], recv_sem=wrecv.at[s],
            device_id=(grp, lax.rem(me + s, n)), device_id_type=mesh_id,
        )

    @pl.loop(1, n)
    def _(s):
        w_copy(s).start()

    @pl.loop(1, n)
    def _(s):
        msg_copy(s).start()

    @pl.loop(1, n)
    def _(s):
        w_copy(s).wait()

    for j in range(n):
        weight_ref[j * own : (j + 1) * own, :] = w_in[lax.rem(me - j + n, n)]

    own_copy.wait()

    @pl.loop(1, n)
    def _(s):
        part_copy(s).wait_send()
        msg_copy(s).wait()


def pair_kernel(
    tiles_step, tile_pairs, station_ref, count_ref, recv_ref, weight_ref, first_ref, second_ref,
    lag_ref, out_ref, rows_ref,
):
    step = pl.program_id(0)
    senders, per_chunk, length = recv_ref.shape
    half = length // 2
    sub = 8
    wide = recv_ref[...].astype(jnp.float32)
    for h in range(per_chunk // sub):
        rows_ref[h] = (
            wide[:, h * sub : (h + 1) * sub, :].reshape(senders * sub, length).astype(jnp.bfloat16)
        )
    live_id = lax.broadcasted_iota(jnp.int32, (tile_pairs, out_ref.shape[1]), 0)
    slot_id = lax.broadcasted_iota(jnp.int32, (senders * sub, tile_pairs), 0)
    slots = station_ref.shape[0]

    @pl.loop(0, tiles_step)
    def _(i):
        tile = step * tiles_step + i
        h = i // sub
        k = lax.rem(i, sub)

        def member(ref):
            place = (ref[pl.ds(i, 1), :] // slots) * sub + k
            pick = (slot_id == place).astype(jnp.float32).astype(jnp.bfloat16)
            return lax.dot_general(
                pick, rows_ref[h], (((0,), (0,)), ((), ())), preferred_element_type=jnp.float32
            )

        a, b = member(first_ref), member(second_ref)
        w = weight_ref[pl.ds(station_ref[tile], 1), :]
        a_re, a_im, b_re, b_im = a[:, :half], a[:, half:], b[:, :half], b[:, half:]
        cross = jnp.concatenate(
            [
                ((a_re * b_re + a_im * b_im) * w).astype(jnp.bfloat16),
                ((a_im * b_re - a_re * b_im) * w).astype(jnp.bfloat16),
            ],
            axis=1,
        )
        lagged = jnp.dot(cross, lag_ref[...], preferred_element_type=jnp.float32)
        row = pl.multiple_of(i * tile_pairs, tile_pairs)
        out_ref[pl.ds(row, tile_pairs), :] = jnp.where(live_id < count_ref[tile], lagged, 0.0)


def shards(windows, rotation, source_inverse, send_rows, tile_station, tile_count, pair_rows):
    ev_dev, comps, stations, length = windows.shape
    half = length // 2
    n = lax.axis_size("ev")
    cap = send_rows.shape[1]
    own = stations // n
    dma = pltpu.SemaphoreType.DMA
    vmem = pl.BlockSpec(memory_space=pltpu.VMEM)
    received, weight = pl.pallas_call(
        partial(exchange_kernel, n, ev_dev * n),
        out_shape=(
            jax.ShapeDtypeStruct((n, cap, length), jnp.bfloat16),
            jax.ShapeDtypeStruct((stations, half), jnp.float32),
        ),
        in_specs=[vmem] * 5,
        out_specs=(pl.BlockSpec(memory_space=pl.ANY), vmem),
        scratch_shapes=[
            pltpu.VMEM((ev_dev * stations, length), jnp.bfloat16),
            pltpu.VMEM((stations, half), jnp.float32),
            pltpu.VMEM((n, cap, length), jnp.bfloat16),
            pltpu.VMEM((n, own, half), jnp.float32),
            pltpu.VMEM((n, own, half), jnp.float32),
            pltpu.VMEM((n, own, half), jnp.float32),
            dma((n,)), dma((n,)), dma((n,)), dma((n,)), dma((n,)), dma((n,)), dma,
        ],
        compiler_params=pltpu.CompilerParams(
            collective_id=0, has_side_effects=True, vmem_limit_bytes=40 << 20
        ),
        name="exchange",
    )(
        windows, rotation, source_inverse, send_rows.reshape(n // GROUP, GROUP * cap),
        spectral_table(length),
    )

    tiles = tile_station.shape[0]
    tile_pairs = pair_rows.shape[1] // tiles
    senders = n * cap // tiles
    received = received.reshape(senders, tiles, length)
    step = 16
    members = pair_rows.reshape(2, tiles, tile_pairs)
    smem = pl.BlockSpec(memory_space=pltpu.SMEM)
    return pl.pallas_call(
        partial(pair_kernel, step, tile_pairs),
        grid=(tiles // step,),
        out_shape=jax.ShapeDtypeStruct((tiles * tile_pairs, LAGS), jnp.float32),
        in_specs=[
            smem,
            smem,
            pl.BlockSpec((senders, step, length), lambda i: (0, i, 0)),
            pl.BlockSpec((stations, half), lambda i: (0, 0)),
            pl.BlockSpec((None, step, tile_pairs), lambda i: (0, i, 0)),
            pl.BlockSpec((None, step, tile_pairs), lambda i: (1, i, 0)),
            pl.BlockSpec((length, LAGS), lambda i: (0, 0)),
        ],
        out_specs=pl.BlockSpec((step * tile_pairs, LAGS), lambda i: (i, 0)),
        scratch_shapes=[pltpu.VMEM((step // 8, senders * 8, length), jnp.bfloat16)],
        compiler_params=pltpu.CompilerParams(vmem_limit_bytes=48 << 20),
        name="pairs",
    )(tile_station, tile_count, received, weight, members, members, lag_table(length, LAGS))


def solution(mesh):
    in_specs = (
        P(("grp", "ev"), None, None, None),
        P(("grp", "ev"), None, None),
        P(("grp", "ev"), None),
        P(("grp", "ev"), None),
        P(("grp", "ev")),
        P(("grp", "ev")),
        P(None, ("grp", "ev")),
    )
    out_specs = P(("grp", "ev"), None)
    return jax.shard_map(shards, mesh=mesh, in_specs=in_specs, out_specs=out_specs, check_vma=False)
```

```python
from functools import partial
import math

import jax
import jax.numpy as jnp
import numpy as np
from jax import lax
from jax.experimental import pallas as pl
from jax.experimental.pallas import tpu as pltpu
from jax.sharding import PartitionSpec as P

LAGS = 255
GROUP = 8
epsilon = 1e-06


def spectral_table(length):
    half_len = length // 2
    samples = np.arange(length, dtype=np.int32)[:, None]
    frequency = np.arange(half_len, dtype=np.int32)[None, :]
    angles = (samples * frequency % length).astype(np.float32) * np.float32(2.0 * math.pi / length)
    factor = np.float32(1.0 / math.sqrt(length))
    return jnp.asarray(
        np.concatenate([np.cos(angles) * factor, -np.sin(angles) * factor], axis=1), jnp.bfloat16
    )


def lag_table(length, lag_count):
    half_len = length // 2
    frequency = np.arange(half_len, dtype=np.int32)[:, None]
    shifts = np.arange(lag_count, dtype=np.int32)[None, :] - lag_count // 2
    angles = (frequency * shifts % length).astype(np.float32) * np.float32(2.0 * math.pi / length)
    factor = np.float32(1.0 / math.sqrt(half_len))
    return jnp.asarray(
        np.concatenate([np.cos(angles) * factor, -np.sin(angles) * factor], axis=0), jnp.bfloat16
    )


def exchange_kernel(
    n, events_total, win_ref, rot_ref, inv_ref, send_ref, table_ref,
    recv_ref, weight_ref,
    spectra, power, msg, part_out, part_in, w_in, far_spectra, far_send, far_msg,
    send_sem, recv_sem, psend, precv, wsend, wrecv, fsend, frecv, rsend, isem, local_sem,
):
    me = lax.axis_index("ev")
    grp = lax.axis_index("grp")
    mesh_id = pl.DeviceIdType.MESH
    ev_dev, comps, stations, length = win_ref.shape
    half = length // 2
    cap = recv_ref.shape[1]
    own = stations // n
    near = n // 2
    side = me // near
    base = side * near
    quarter = me // (n // 4)
    inner = (quarter == 1) | (quarter == 2)
    partner = lax.rem(me + n // 4 + side * near, n)

    def remote(src, dst, ssem, rsem, target):
        return pltpu.make_async_remote_copy(
            src_ref=src, dst_ref=dst, send_sem=ssem, recv_sem=rsem,
            device_id=(grp, target), device_id_type=mesh_id,
        )

    barrier = pltpu.get_barrier_semaphore()

    @pl.loop(1, n)
    def _(s):
        pl.semaphore_signal(
            barrier, inc=1, device_id=(grp, lax.rem(me + s, n)), device_id_type=mesh_id
        )

    power[...] = jnp.zeros_like(power)
    diag = lax.broadcasted_iota(jnp.int32, (stations, stations), 0) == lax.broadcasted_iota(
        jnp.int32, (stations, stations), 1
    )
    inv_all = inv_ref[...].astype(jnp.float32)
    event_id = lax.broadcasted_iota(jnp.int32, (ev_dev, length), 0)
    pl.semaphore_wait(barrier, n - 1)

    def index_copy():
        return remote(send_ref, far_send, isem.at[0], isem.at[1], partner)

    def far_copy(e):
        row = pl.ds(pl.multiple_of(e * stations, stations), stations)
        return remote(spectra.at[row], far_spectra.at[row], fsend.at[e], frecv.at[e], partner)

    @pl.when(inner)
    def _():
        index_copy().start()

    @pl.loop(0, ev_dev)
    def _(e):
        rot = rot_ref[e].astype(jnp.float32)
        acc = None
        for c in range(comps):
            col = jnp.sum(
                jnp.where(diag, jnp.broadcast_to(rot[c : c + 1, :], diag.shape), 0.0),
                axis=1, keepdims=True,
            )
            term = col * win_ref[e, c].astype(jnp.float32)
            acc = term if acc is None else acc + term
        spec = jnp.dot(
            acc.astype(jnp.bfloat16), table_ref[...], preferred_element_type=jnp.float32
        )
        gain = jnp.sum(jnp.where(event_id == e, inv_all, 0.0), axis=0, keepdims=True)
        re, im = spec[:, :half], spec[:, half:]
        g_re, g_im = gain[:, :half], gain[:, half:]
        d_re = re * g_re - im * g_im
        d_im = re * g_im + im * g_re
        power[...] += d_re * d_re + d_im * d_im
        row = pl.multiple_of(e * stations, stations)
        spectra[pl.ds(row, stations), :half] = d_re.astype(jnp.bfloat16)
        spectra[pl.ds(row, stations), half:] = d_im.astype(jnp.bfloat16)

        @pl.when(inner)
        def _():
            far_copy(e).start()

    for j in range(n):
        part_out[j] = power[j * own : (j + 1) * own, :]

    def part_copy(s):
        target = lax.rem(me + s, n)
        return remote(part_out.at[target], part_in.at[s], psend.at[s], precv.at[s], target)

    @pl.loop(1, n)
    def _(s):
        part_copy(s).start()

    rows = ev_dev * stations
    row_id = lax.broadcasted_iota(jnp.int32, (rows, GROUP * cap), 0)

    def gather(index_ref, from_ref, to_ref, g, place):
        pick = (row_id == index_ref[pl.ds(g, 1), :]).astype(jnp.float32).astype(jnp.bfloat16)
        got = lax.dot_general(
            pick, from_ref[...], (((0,), (0,)), ((), ())), preferred_element_type=jnp.float32
        )
        to_ref[pl.ds(pl.multiple_of(place, GROUP), GROUP)] = got.astype(jnp.bfloat16).reshape(
            GROUP, cap, length
        )

    def msg_copy(target):
        return remote(
            msg.at[target], recv_ref.at[me], send_sem.at[target], recv_sem.at[me], target
        )

    def near_target(s):
        return base + lax.rem(me - base + s, near)

    def far_target(s):
        return near - base + lax.rem(me - base + s, near)

    side_groups = near // GROUP

    @pl.loop(0, side_groups)
    def _(i):
        g = side * side_groups + i
        gather(send_ref, spectra, msg, g, g * GROUP)

    own_copy = pltpu.make_async_copy(msg.at[me], recv_ref.at[me], local_sem.at[0])
    own_copy.start()

    @pl.loop(1, near)
    def _(s):
        msg_copy(near_target(s)).start()

    @pl.when(jnp.logical_not(inner))
    def _():
        @pl.loop(0, side_groups)
        def _(i):
            g = (1 - side) * side_groups + i
            gather(send_ref, spectra, msg, g, g * GROUP)

        @pl.loop(0, near)
        def _(s):
            msg_copy(far_target(s)).start()

    @pl.loop(1, n)
    def _(s):
        part_copy(s).wait_recv()

    total = part_out[me]
    for s in range(1, n):
        total = total + part_in[s]
    w_in[0] = 1.0 / (total / events_total + epsilon)

    def w_copy(s):
        return remote(w_in.at[0], w_in.at[s], wsend.at[s], wrecv.at[s], lax.rem(me + s, n))

    @pl.loop(1, n)
    def _(s):
        w_copy(s).start()

    def relay_copy(target):
        return remote(
            far_msg.at[target - base], recv_ref.at[partner], rsend.at[target - base],
            recv_sem.at[partner], target,
        )

    def partner_copy():
        return pltpu.make_async_copy(
            far_msg.at[me - base], recv_ref.at[partner], local_sem.at[1]
        )

    @pl.when(inner)
    def _():
        index_copy().wait()

        @pl.loop(0, ev_dev)
        def _(e):
            far_copy(e).wait()

        @pl.loop(0, side_groups)
        def _(i):
            gather(far_send, far_spectra, far_msg, side * side_groups + i, i * GROUP)

        partner_copy().start()

        @pl.loop(1, near)
        def _(s):
            relay_copy(near_target(s)).start()

    @pl.loop(1, n)
    def _(s):
        w_copy(s).wait()

    for j in range(n):
        weight_ref[j * own : (j + 1) * own, :] = w_in[lax.rem(me - j + n, n)]

    own_copy.wait()

    @pl.loop(1, n)
    def _(s):
        part_copy(s).wait_send()

    def arrived(source):
        remote(
            msg.at[source], recv_ref.at[source], send_sem.at[source], recv_sem.at[source], source
        ).wait_recv()

    @pl.loop(1, near)
    def _(s):
        msg_copy(near_target(s)).wait_send()
        arrived(near_target(s))

    @pl.when(jnp.logical_not(inner))
    def _():
        @pl.loop(0, near)
        def _(s):
            msg_copy(far_target(s)).wait_send()
            arrived(far_target(s))

    @pl.when(inner)
    def _():
        partner_copy().wait()

        @pl.loop(0, near)
        def _(s):
            source = far_target(s)

            @pl.when(source != partner)
            def _():
                arrived(source)

        @pl.loop(1, near)
        def _(s):
            relay_copy(near_target(s)).wait_send()


def pair_kernel(
    batch, tile_pairs, station_ref, count_ref, recv_ref, weight_ref, first_ref, second_ref,
    lag_ref, out_ref, rows_ref, cross_ref,
):
    senders, per_step, length = recv_ref.shape
    first_tile = pl.program_id(0) * per_step
    half = length // 2
    sub = 8
    width = half // 2
    slots = station_ref.shape[0]
    wide = recv_ref[...].astype(jnp.float32)
    for h in range(per_step // sub):
        rows_ref[h] = (
            wide[:, h * sub : (h + 1) * sub, :].reshape(senders * sub, length).astype(jnp.bfloat16)
        )
    live_id = lax.broadcasted_iota(jnp.int32, (tile_pairs, out_ref.shape[1]), 0)
    lane = lax.broadcasted_iota(jnp.int32, (tile_pairs, senders * sub), 1)

    def places(ref):
        r = ref[...]
        k = lax.rem(lax.broadcasted_iota(jnp.int32, r.shape, 0), sub)
        return jnp.transpose((r // slots) * sub + k)

    def pick(place, t0):
        return jnp.concatenate(
            [
                (lane == place[:, t : t + 1]).astype(jnp.float32).astype(jnp.bfloat16)
                for t in range(t0, t0 + batch)
            ],
            axis=0,
        )

    first, second = places(first_ref), places(second_ref)
    for t0 in range(0, per_step, batch):
        h = t0 // sub
        pick_a, pick_b = pick(first, t0), pick(second, t0)
        for c in range(0, half, width):

            def member(picked, at):
                return jnp.dot(
                    picked, rows_ref[h, :, at : at + width], preferred_element_type=jnp.float32
                )

            a_re, a_im = member(pick_a, c), member(pick_a, half + c)
            b_re, b_im = member(pick_b, c), member(pick_b, half + c)
            re = a_re * b_re + a_im * b_im
            im = a_im * b_re - a_re * b_im
            for j in range(batch):
                station = station_ref[first_tile + t0 + j]
                w = weight_ref[pl.ds(station, 1), c : c + width]
                at = slice(j * tile_pairs, (j + 1) * tile_pairs)
                cross_ref[at, c : c + width] = (re[at] * w).astype(jnp.bfloat16)
                cross_ref[at, half + c : half + c + width] = (im[at] * w).astype(jnp.bfloat16)
        lagged = jnp.dot(cross_ref[...], lag_ref[...], preferred_element_type=jnp.float32)
        for j in range(batch):
            at = (t0 + j) * tile_pairs
            out_ref[at : at + tile_pairs, :] = jnp.where(
                live_id < count_ref[first_tile + t0 + j],
                lagged[j * tile_pairs : (j + 1) * tile_pairs], 0.0,
            )


def shards(windows, rotation, source_inverse, send_rows, tile_station, tile_count, pair_rows):
    ev_dev, comps, stations, length = windows.shape
    half = length // 2
    n = lax.axis_size("ev")
    cap = send_rows.shape[1]
    own = stations // n
    dma = pltpu.SemaphoreType.DMA
    vmem = pl.BlockSpec(memory_space=pltpu.VMEM)
    received, weight = pl.pallas_call(
        partial(exchange_kernel, n, ev_dev * n),
        out_shape=(
            jax.ShapeDtypeStruct((n, cap, length), jnp.bfloat16),
            jax.ShapeDtypeStruct((stations, half), jnp.float32),
        ),
        in_specs=[vmem] * 5,
        out_specs=(pl.BlockSpec(memory_space=pl.ANY), vmem),
        scratch_shapes=[
            pltpu.VMEM((ev_dev * stations, length), jnp.bfloat16),
            pltpu.VMEM((stations, half), jnp.float32),
            pltpu.VMEM((n, cap, length), jnp.bfloat16),
            pltpu.VMEM((n, own, half), jnp.float32),
            pltpu.VMEM((n, own, half), jnp.float32),
            pltpu.VMEM((n, own, half), jnp.float32),
            pltpu.VMEM((ev_dev * stations, length), jnp.bfloat16),
            pltpu.VMEM((n // GROUP, GROUP * cap), jnp.int32),
            pltpu.VMEM((n // 2, cap, length), jnp.bfloat16),
            dma((n,)), dma((n,)), dma((n,)), dma((n,)), dma((n,)), dma((n,)),
            dma((ev_dev,)), dma((ev_dev,)), dma((n // 2,)), dma((2,)), dma((2,)),
        ],
        compiler_params=pltpu.CompilerParams(
            collective_id=0, has_side_effects=True, vmem_limit_bytes=40 << 20
        ),
        name="exchange",
    )(
        windows, rotation, source_inverse, send_rows.reshape(n // GROUP, GROUP * cap),
        spectral_table(length),
    )

    tiles = tile_station.shape[0]
    tile_pairs = pair_rows.shape[1] // tiles
    senders = n * cap // tiles
    received = received.reshape(senders, tiles, length)
    step, batch = 16, 4
    members = pair_rows.reshape(2, tiles, tile_pairs)
    smem = pl.BlockSpec(memory_space=pltpu.SMEM)
    return pl.pallas_call(
        partial(pair_kernel, batch, tile_pairs),
        grid=(tiles // step,),
        out_shape=jax.ShapeDtypeStruct((tiles * tile_pairs, LAGS), jnp.float32),
        in_specs=[
            smem,
            smem,
            pl.BlockSpec((senders, step, length), lambda i: (0, i, 0)),
            pl.BlockSpec((stations, half), lambda i: (0, 0)),
            pl.BlockSpec((None, step, tile_pairs), lambda i: (0, i, 0)),
            pl.BlockSpec((None, step, tile_pairs), lambda i: (1, i, 0)),
            pl.BlockSpec((length, LAGS), lambda i: (0, 0)),
        ],
        out_specs=pl.BlockSpec((step * tile_pairs, LAGS), lambda i: (i, 0)),
        scratch_shapes=[
            pltpu.VMEM((step // 8, senders * 8, length), jnp.bfloat16),
            pltpu.VMEM((batch * tile_pairs, length), jnp.bfloat16),
        ],
        compiler_params=pltpu.CompilerParams(vmem_limit_bytes=48 << 20),
        name="pairs",
    )(tile_station, tile_count, received, weight, members, members, lag_table(length, LAGS))


def solution(mesh):
    in_specs = (
        P(("grp", "ev"), None, None, None),
        P(("grp", "ev"), None, None),
        P(("grp", "ev"), None),
        P(("grp", "ev"), None),
        P(("grp", "ev")),
        P(("grp", "ev")),
        P(None, ("grp", "ev")),
    )
    out_specs = P(("grp", "ev"), None)
    return jax.shard_map(shards, mesh=mesh, in_specs=in_specs, out_specs=out_specs, check_vma=False)
```

```python
from functools import partial
import math

import jax
import jax.numpy as jnp
import numpy as np
from jax import lax
from jax.experimental import pallas as pl
from jax.experimental.pallas import tpu as pltpu
from jax.sharding import PartitionSpec as P

LAGS = 255
GROUP = 8
epsilon = 1e-06


def spectral_table(length):
    half_len = length // 2
    samples = np.arange(length, dtype=np.int32)[:, None]
    frequency = np.arange(half_len, dtype=np.int32)[None, :]
    angles = (samples * frequency % length).astype(np.float32) * np.float32(2.0 * math.pi / length)
    factor = np.float32(1.0 / math.sqrt(length))
    return jnp.asarray(
        np.concatenate([np.cos(angles) * factor, -np.sin(angles) * factor], axis=1), jnp.bfloat16
    )


def lag_table(length, lag_count):
    half_len = length // 2
    frequency = np.arange(half_len, dtype=np.int32)[:, None]
    shifts = np.arange(lag_count, dtype=np.int32)[None, :] - lag_count // 2
    angles = (frequency * shifts % length).astype(np.float32) * np.float32(2.0 * math.pi / length)
    factor = np.float32(1.0 / math.sqrt(half_len))
    return jnp.asarray(
        np.concatenate([np.cos(angles) * factor, -np.sin(angles) * factor], axis=0), jnp.bfloat16
    )


def exchange_kernel(
    n, events_total, win_hbm, rot_ref, inv_ref, send_ref, table_hbm,
    recv_ref, weight_ref,
    spectra, power, msg, part_out, part_in, w_in, far_spectra, far_send, far_msg,
    win_ref, table_ref,
    send_sem, recv_sem, psend, precv, wsend, wrecv, fsend, frecv, rsend, isem, local_sem, load_sem,
):
    me = lax.axis_index("ev")
    grp = lax.axis_index("grp")
    mesh_id = pl.DeviceIdType.MESH
    ev_dev, comps, stations, length = win_hbm.shape
    half = length // 2
    cap = recv_ref.shape[1]
    own = stations // n
    near = n // 2
    side = me // near
    base = side * near
    quarter = me // (n // 4)
    inner = (quarter == 1) | (quarter == 2)
    partner = lax.rem(me + n // 4 + side * near, n)

    def remote(src, dst, ssem, rsem, target):
        return pltpu.make_async_remote_copy(
            src_ref=src, dst_ref=dst, send_sem=ssem, recv_sem=rsem,
            device_id=(grp, target), device_id_type=mesh_id,
        )

    barrier = pltpu.get_barrier_semaphore()

    @pl.loop(1, n)
    def _(s):
        pl.semaphore_signal(
            barrier, inc=1, device_id=(grp, lax.rem(me + s, n)), device_id_type=mesh_id
        )

    def win_copy(e):
        return pltpu.make_async_copy(win_hbm.at[e], win_ref.at[e], load_sem.at[e])

    table_copy = pltpu.make_async_copy(table_hbm, table_ref, load_sem.at[ev_dev])
    win_copy(0).start()
    table_copy.start()

    @pl.loop(1, ev_dev)
    def _(e):
        win_copy(e).start()

    power[...] = jnp.zeros_like(power)
    diag = lax.broadcasted_iota(jnp.int32, (stations, stations), 0) == lax.broadcasted_iota(
        jnp.int32, (stations, stations), 1
    )
    inv_all = inv_ref[...].astype(jnp.float32)
    event_id = lax.broadcasted_iota(jnp.int32, (ev_dev, length), 0)
    pl.semaphore_wait(barrier, n - 1)

    def index_copy():
        return remote(send_ref, far_send, isem.at[0], isem.at[1], partner)

    def far_copy(e):
        row = pl.ds(pl.multiple_of(e * stations, stations), stations)
        return remote(spectra.at[row], far_spectra.at[row], fsend.at[e], frecv.at[e], partner)

    @pl.when(inner)
    def _():
        index_copy().start()

    table_copy.wait()

    @pl.loop(0, ev_dev)
    def _(e):
        win_copy(e).wait()
        rot = rot_ref[e].astype(jnp.float32)
        acc = None
        for c in range(comps):
            col = jnp.sum(
                jnp.where(diag, jnp.broadcast_to(rot[c : c + 1, :], diag.shape), 0.0),
                axis=1, keepdims=True,
            )
            term = col * win_ref[e, c].astype(jnp.float32)
            acc = term if acc is None else acc + term
        spec = jnp.dot(
            acc.astype(jnp.bfloat16), table_ref[...], preferred_element_type=jnp.float32
        )
        gain = jnp.sum(jnp.where(event_id == e, inv_all, 0.0), axis=0, keepdims=True)
        re, im = spec[:, :half], spec[:, half:]
        g_re, g_im = gain[:, :half], gain[:, half:]
        d_re = re * g_re - im * g_im
        d_im = re * g_im + im * g_re
        power[...] += d_re * d_re + d_im * d_im
        row = pl.multiple_of(e * stations, stations)
        spectra[pl.ds(row, stations), :half] = d_re.astype(jnp.bfloat16)
        spectra[pl.ds(row, stations), half:] = d_im.astype(jnp.bfloat16)

        @pl.when(inner)
        def _():
            far_copy(e).start()

    for j in range(n):
        part_out[j] = power[j * own : (j + 1) * own, :]

    def part_copy(s):
        target = lax.rem(me + s, n)
        return remote(part_out.at[target], part_in.at[s], psend.at[s], precv.at[s], target)

    @pl.loop(1, n)
    def _(s):
        part_copy(s).start()

    rows = ev_dev * stations
    row_id = lax.broadcasted_iota(jnp.int32, (rows, GROUP * cap), 0)

    def gather(index_ref, from_ref, to_ref, g, place):
        wanted = jnp.concatenate(
            [index_ref[pl.ds(g * GROUP + r, 1), :] for r in range(GROUP)], axis=1
        )
        pick = (row_id == wanted).astype(jnp.float32).astype(jnp.bfloat16)
        got = lax.dot_general(
            pick, from_ref[...], (((0,), (0,)), ((), ())), preferred_element_type=jnp.float32
        )
        to_ref[pl.ds(pl.multiple_of(place, GROUP), GROUP)] = got.astype(jnp.bfloat16).reshape(
            GROUP, cap, length
        )

    def msg_copy(target):
        return remote(
            msg.at[target], recv_ref.at[me], send_sem.at[target], recv_sem.at[me], target
        )

    def near_target(s):
        return base + lax.rem(me - base + s, near)

    def far_target(s):
        return near - base + lax.rem(me - base + s, near)

    side_groups = near // GROUP

    @pl.loop(0, side_groups)
    def _(i):
        g = side * side_groups + i
        gather(send_ref, spectra, msg, g, g * GROUP)

    own_copy = pltpu.make_async_copy(msg.at[me], recv_ref.at[me], local_sem.at[0])
    own_copy.start()

    @pl.loop(1, near)
    def _(s):
        msg_copy(near_target(s)).start()

    @pl.when(jnp.logical_not(inner))
    def _():
        @pl.loop(0, side_groups)
        def _(i):
            g = (1 - side) * side_groups + i
            gather(send_ref, spectra, msg, g, g * GROUP)

        @pl.loop(0, near)
        def _(s):
            msg_copy(far_target(s)).start()

    @pl.loop(1, n)
    def _(s):
        part_copy(s).wait_recv()

    total = part_out[me]
    for s in range(1, n):
        total = total + part_in[s]
    w_in[0] = 1.0 / (total / events_total + epsilon)

    def w_copy(s):
        return remote(w_in.at[0], w_in.at[s], wsend.at[s], wrecv.at[s], lax.rem(me + s, n))

    @pl.loop(1, n)
    def _(s):
        w_copy(s).start()

    def relay_copy(target):
        return remote(
            far_msg.at[target - base], recv_ref.at[partner], rsend.at[target - base],
            recv_sem.at[partner], target,
        )

    def partner_copy():
        return pltpu.make_async_copy(
            far_msg.at[me - base], recv_ref.at[partner], local_sem.at[1]
        )

    @pl.when(inner)
    def _():
        index_copy().wait()

        @pl.loop(0, ev_dev)
        def _(e):
            far_copy(e).wait()

        @pl.loop(0, side_groups)
        def _(i):
            gather(far_send, far_spectra, far_msg, side * side_groups + i, i * GROUP)

        partner_copy().start()

        @pl.loop(1, near)
        def _(s):
            relay_copy(near_target(s)).start()

    @pl.loop(1, n)
    def _(s):
        w_copy(s).wait()

    for j in range(n):
        weight_ref[j * own : (j + 1) * own, :] = w_in[lax.rem(me - j + n, n)]

    own_copy.wait()

    @pl.loop(1, n)
    def _(s):
        part_copy(s).wait_send()

    def arrived(source):
        remote(
            msg.at[source], recv_ref.at[source], send_sem.at[source], recv_sem.at[source], source
        ).wait_recv()

    @pl.loop(1, near)
    def _(s):
        msg_copy(near_target(s)).wait_send()
        arrived(near_target(s))

    @pl.when(jnp.logical_not(inner))
    def _():
        @pl.loop(0, near)
        def _(s):
            msg_copy(far_target(s)).wait_send()
            arrived(far_target(s))

    @pl.when(inner)
    def _():
        partner_copy().wait()

        @pl.loop(0, near)
        def _(s):
            source = far_target(s)

            @pl.when(source != partner)
            def _():
                arrived(source)

        @pl.loop(1, near)
        def _(s):
            relay_copy(near_target(s)).wait_send()


def pair_kernel(
    batch, tile_pairs, station_ref, count_ref, recv_ref, weight_ref, member_ref,
    lag_ref, out_ref, rows_ref, cross_ref,
):
    senders, per_step, length = recv_ref.shape
    first_tile = pl.program_id(0) * per_step
    half = length // 2
    sub = 8
    width = half // 2
    slots = station_ref.shape[0]
    wide = recv_ref[...].astype(jnp.float32)
    for h in range(per_step // sub):
        rows_ref[h] = (
            wide[:, h * sub : (h + 1) * sub, :].reshape(senders * sub, length).astype(jnp.bfloat16)
        )
    live_id = lax.broadcasted_iota(jnp.int32, (tile_pairs, out_ref.shape[1]), 0)
    lane = lax.broadcasted_iota(jnp.int32, (tile_pairs, senders * sub), 1)

    def places(m):
        r = jnp.concatenate(
            [
                member_ref[m : m + 1, t * tile_pairs : (t + 1) * tile_pairs]
                for t in range(per_step)
            ],
            axis=0,
        )
        k = lax.rem(lax.broadcasted_iota(jnp.int32, r.shape, 0), sub)
        return jnp.transpose((r // slots) * sub + k)

    def pick(place, t0):
        return jnp.concatenate(
            [
                (lane == place[:, t : t + 1]).astype(jnp.float32).astype(jnp.bfloat16)
                for t in range(t0, t0 + batch)
            ],
            axis=0,
        )

    first, second = places(0), places(1)
    for t0 in range(0, per_step, batch):
        h = t0 // sub
        pick_a, pick_b = pick(first, t0), pick(second, t0)
        for c in range(0, half, width):

            def member(picked, at):
                return jnp.dot(
                    picked, rows_ref[h, :, at : at + width], preferred_element_type=jnp.float32
                )

            a_re, a_im = member(pick_a, c), member(pick_a, half + c)
            b_re, b_im = member(pick_b, c), member(pick_b, half + c)
            re = a_re * b_re + a_im * b_im
            im = a_im * b_re - a_re * b_im
            for j in range(batch):
                station = station_ref[first_tile + t0 + j]
                w = weight_ref[pl.ds(station, 1), c : c + width]
                at = slice(j * tile_pairs, (j + 1) * tile_pairs)
                cross_ref[at, c : c + width] = (re[at] * w).astype(jnp.bfloat16)
                cross_ref[at, half + c : half + c + width] = (im[at] * w).astype(jnp.bfloat16)
        lagged = jnp.dot(cross_ref[...], lag_ref[...], preferred_element_type=jnp.float32)
        for j in range(batch):
            at = (t0 + j) * tile_pairs
            out_ref[at : at + tile_pairs, :] = jnp.where(
                live_id < count_ref[first_tile + t0 + j],
                lagged[j * tile_pairs : (j + 1) * tile_pairs], 0.0,
            )


def shards(windows, rotation, source_inverse, send_rows, tile_station, tile_count, pair_rows):
    ev_dev, comps, stations, length = windows.shape
    half = length // 2
    n = lax.axis_size("ev")
    cap = send_rows.shape[1]
    own = stations // n
    dma = pltpu.SemaphoreType.DMA
    vmem = pl.BlockSpec(memory_space=pltpu.VMEM)
    hbm = pl.BlockSpec(memory_space=pltpu.HBM)
    received, weight = pl.pallas_call(
        partial(exchange_kernel, n, ev_dev * n),
        out_shape=(
            jax.ShapeDtypeStruct((n, cap, length), jnp.bfloat16),
            jax.ShapeDtypeStruct((stations, half), jnp.float32),
        ),
        in_specs=[hbm, vmem, vmem, vmem, hbm],
        out_specs=(pl.BlockSpec(memory_space=pl.ANY), vmem),
        scratch_shapes=[
            pltpu.VMEM((ev_dev * stations, length), jnp.bfloat16),
            pltpu.VMEM((stations, half), jnp.float32),
            pltpu.VMEM((n, cap, length), jnp.bfloat16),
            pltpu.VMEM((n, own, half), jnp.float32),
            pltpu.VMEM((n, own, half), jnp.float32),
            pltpu.VMEM((n, own, half), jnp.float32),
            pltpu.VMEM((ev_dev * stations, length), jnp.bfloat16),
            pltpu.VMEM((n, cap), jnp.int32),
            pltpu.VMEM((n // 2, cap, length), jnp.bfloat16),
            pltpu.VMEM((ev_dev, comps, stations, length), jnp.bfloat16),
            pltpu.VMEM((length, length), jnp.bfloat16),
            dma((n,)), dma((n,)), dma((n,)), dma((n,)), dma((n,)), dma((n,)),
            dma((ev_dev,)), dma((ev_dev,)), dma((n // 2,)), dma((2,)), dma((2,)), dma((ev_dev + 1,)),
        ],
        compiler_params=pltpu.CompilerParams(
            collective_id=0, has_side_effects=True, vmem_limit_bytes=40 << 20
        ),
        name="exchange",
    )(
        windows, rotation, source_inverse, send_rows,
        spectral_table(length),
    )

    tiles = tile_station.shape[0]
    tile_pairs = pair_rows.shape[1] // tiles
    senders = n * cap // tiles
    received = received.reshape(senders, tiles, length)
    step, batch = 16, 4
    smem = pl.BlockSpec(memory_space=pltpu.SMEM)
    return pl.pallas_call(
        partial(pair_kernel, batch, tile_pairs),
        grid=(tiles // step,),
        out_shape=jax.ShapeDtypeStruct((tiles * tile_pairs, LAGS), jnp.float32),
        in_specs=[
            smem,
            smem,
            pl.BlockSpec((senders, step, length), lambda i: (0, i, 0)),
            pl.BlockSpec((stations, half), lambda i: (0, 0)),
            pl.BlockSpec((2, step * tile_pairs), lambda i: (0, i)),
            pl.BlockSpec((length, LAGS), lambda i: (0, 0)),
        ],
        out_specs=pl.BlockSpec((step * tile_pairs, LAGS), lambda i: (i, 0)),
        scratch_shapes=[
            pltpu.VMEM((step // 8, senders * 8, length), jnp.bfloat16),
            pltpu.VMEM((batch * tile_pairs, length), jnp.bfloat16),
        ],
        compiler_params=pltpu.CompilerParams(vmem_limit_bytes=48 << 20),
        name="pairs",
    )(tile_station, tile_count, received, weight, pair_rows, lag_table(length, LAGS))


def solution(mesh):
    in_specs = (
        P(("grp", "ev"), None, None, None),
        P(("grp", "ev"), None, None),
        P(("grp", "ev"), None),
        P(("grp", "ev"), None),
        P(("grp", "ev")),
        P(("grp", "ev")),
        P(None, ("grp", "ev")),
    )
    out_specs = P(("grp", "ev"), None)
    return jax.shard_map(shards, mesh=mesh, in_specs=in_specs, out_specs=out_specs, check_vma=False)
```
